32 devices in a mesh: ctx: 8 (over y, x, core), head: 4 (over z).
Axes of the slice: x: 2, y: 2, z: 4, core: 2. Of those that a mesh axis runs over, the one named last changes fastest.
Arguments:
- queries: bfloat16 [16384, 8, 128], P('ctx', 'head'), may hold values from -100 to 100
- key_vectors: bfloat16 [16384, 128], P('ctx'), may hold values from -41 to 41
- value_vectors: bfloat16 [16384, 128], P('ctx'), may hold values from -24 to 24
- grad_out: bfloat16 [16384, 8, 128], P('ctx', 'head'), may hold values from -6 to 6
- doc_lengths: int32 [10], replicated, may hold values from 1 to 4096, 16384 in all
Outputs:
- attention_out: bfloat16 [16384, 8, 128], P('ctx', 'head')
- grad_queries: bfloat16 [16384, 8, 128], P('ctx', 'head')
- grad_keys: bfloat16 [16384, 128], P(('ctx', 'head'))
- grad_values: bfloat16 [16384, 128], P(('ctx', 'head'))
The draws below stay inside these ranges and needn't reach their ends.
Inputs may be any that keep to these rules, and one draw needn't show every extreme that they name: `doc_lengths`: lengths of the packed documents in sequence order; they sum to 16384 and the longest is exactly 4096.
All inputs are finite; a program needn't handle non-finite values.
Results may differ from the reference program's by a relative error of at most 0.012.
Values may be sent and summed in bfloat16 or wider, within the bound.
A program may use at most 192 MiB of HBM per device.

```python
import math
import jax
import jax.numpy as jnp
import numpy as np
from jax import lax

H = 8
HEAD_DIM = 128
MAXDOC = 4096
TOKENS = 16384
STRETCHES = 16
STRETCH = 1024
REACH = 4
NDOCS = 10


def base_field(key, array_shape):
    return jnp.clip(4.0 * jax.random.normal(key, array_shape, jnp.float32), -24.0, 24.0)


def draw_queries(key, part):
    drawn = base_field(jax.random.fold_in(key, 11), (TOKENS, H, HEAD_DIM))
    return drawn.astype(jnp.bfloat16)


def draw_key_vectors(key, part):
    drawn = base_field(jax.random.fold_in(key, 17), (TOKENS, HEAD_DIM))
    return drawn.astype(jnp.bfloat16)


def shard_levels(rng, shape, cuts, smallest, largest):
    loudness, own = 1.0, jax.random.fold_in(rng, 6)
    for dim, parts in cuts:
        draws = jnp.exp(jax.random.uniform(jax.random.fold_in(own, dim), (parts,), jnp.float32, smallest / len(cuts), largest / len(cuts)))
        loudness = loudness * jnp.repeat(draws, shape[dim] // parts).reshape([-1 if axis == dim else 1 for axis in range(len(shape))])
    return loudness


def split_up(amount, total, limit, skew):
    portions = [(1 << 20) // math.isqrt(rank ** skew) + 1 for rank in range(2, amount + 1)]
    rest, counts = total - limit - (amount - 1), [1] * (amount - 1)
    while rest > 0:
        movable = [i for i in range(amount - 1) if counts[i] < limit]
        whole, left = sum([portions[i] for i in movable]), rest
        for i in movable:
            more = min(limit - counts[i], max(1, left * portions[i] // whole), rest)
            counts[i] = counts[i] + more
            rest = rest - more
    return np.array([limit] + counts)


def uneven_parts(key, count, total, bound, slope):
    if count == 2:
        one = jax.random.randint(key, (), max(1, total - bound), min(bound, total - 1) + 1)
        return jnp.stack([one, total - one])
    sizes = jnp.asarray(split_up(count, total, bound, slope), jnp.int32)
    pairs = (count - 1) // 2
    donor, taker = sizes[1:1 + 2 * pairs:2], sizes[2:2 + 2 * pairs:2]
    room = jnp.minimum(donor - 1, bound - taker)
    shifted = jax.random.randint(jax.random.fold_in(key, 1), (pairs,), 0, 1 << 20) % (room + 1)
    sizes = sizes.at[1:1 + 2 * pairs:2].set(donor - shifted).at[2:2 + 2 * pairs:2].set(taker + shifted)
    return sizes[jax.random.permutation(jax.random.fold_in(key, 2), count)]


def centred(key, extent, deviation, most, split=(), kind=jnp.bfloat16):
    level = shard_levels(key, extent, split, -0.22, 0.18) if split else 1.0
    entries = jax.random.normal(key, extent, jnp.float32) * deviation * level
    return jnp.minimum(jnp.maximum(entries, -most), most).astype(kind)


def setup_inputs(seed: int = 0) -> dict:
    arg_keys = jax.random.split(jax.random.key(seed), 6)
    return {
        "queries": draw_queries(jax.random.fold_in(arg_keys[5], 71), 0),
        "key_vectors": draw_key_vectors(jax.random.fold_in(arg_keys[5], 71), 0),
        "value_vectors": centred(arg_keys[2], (TOKENS, HEAD_DIM), 4.0, 24.0, ((0, 8),)),
        "grad_out": centred(arg_keys[3], (TOKENS, H, HEAD_DIM), 1.0, 6.0, ((0, 8), (1, 4))),
        "doc_lengths": uneven_parts(arg_keys[4], NDOCS, TOKENS, MAXDOC, 1).astype(jnp.int32),
    }


masked_value = -1.0e30


def arranged_block(stretch_total):
    layout = []
    half_total = stretch_total // 2
    for stretch_index in range(stretch_total):
        if stretch_index < half_total:
            layout.append(2 * stretch_index)
        else:
            layout.append(2 * (stretch_total - 1 - stretch_index) + 1)
    return np.array(layout, dtype=np.int32)


def doc_number(positions, doc_ends):
    return jnp.sum((doc_ends[None, :] <= positions[:, None]).astype(jnp.int32), axis=1)


def reference(queries, key_vectors, value_vectors, grad_out, doc_lengths):
    layout = arranged_block(STRETCHES)
    inverse = np.argsort(layout)
    seq_queries = queries.reshape(STRETCHES, STRETCH, H, HEAD_DIM)[layout].reshape(TOKENS, H, HEAD_DIM)
    seq_dout = grad_out.reshape(STRETCHES, STRETCH, H, HEAD_DIM)[layout].reshape(TOKENS, H, HEAD_DIM)
    seq_keys = key_vectors.reshape(STRETCHES, STRETCH, HEAD_DIM)[layout].reshape(TOKENS, HEAD_DIM)
    seq_values = value_vectors.reshape(STRETCHES, STRETCH, HEAD_DIM)[layout].reshape(TOKENS, HEAD_DIM)
    margin = REACH * STRETCH
    span_rows = margin + STRETCH
    padded_keys = jnp.concatenate([jnp.zeros((margin, HEAD_DIM), key_vectors.dtype), seq_keys], axis=0)
    padded_values = jnp.concatenate([jnp.zeros((margin, HEAD_DIM), value_vectors.dtype), seq_values], axis=0)
    doc_ends = jnp.cumsum(doc_lengths).astype(jnp.int32)
    scale_factor = 1.0 / HEAD_DIM

    def visit(carried, stretch_index):
        grad_keys, grad_values = carried
        start = stretch_index * STRETCH
        query_block = lax.dynamic_slice_in_dim(seq_queries, start, STRETCH, 0).astype(jnp.float32)
        dout_block = lax.dynamic_slice_in_dim(seq_dout, start, STRETCH, 0).astype(jnp.float32)
        key_block = lax.dynamic_slice_in_dim(padded_keys, start, span_rows, 0).astype(jnp.float32)
        value_block = lax.dynamic_slice_in_dim(padded_values, start, span_rows, 0).astype(jnp.float32)
        key_pos = start - margin + jnp.arange(span_rows, dtype=jnp.int32)
        query_pos = start + jnp.arange(STRETCH, dtype=jnp.int32)
        key_doc = doc_number(key_pos, doc_ends)
        query_doc = doc_number(query_pos, doc_ends)
        allowed = (key_doc[None, :] == query_doc[:, None]) & (key_pos[None, :] <= query_pos[:, None]) & (key_pos[None, :] >= 0)
        allowed_heads = allowed[None]
        logits = jnp.einsum("chd,kd->hck", query_block, key_block) * scale_factor
        row_max = jnp.max(jnp.where(allowed_heads, logits, masked_value), axis=2)
        row_sum = jnp.sum(jnp.where(allowed_heads, jnp.exp(logits - row_max[..., None]), 0.0), axis=2)
        log_total = row_max + jnp.log(row_sum)
        probs_full = jnp.where(allowed_heads, jnp.exp(logits - log_total[..., None]), 0.0)
        probs_low = lax.optimization_barrier(probs_full.astype(jnp.bfloat16)).astype(jnp.float32)
        out_block = jnp.einsum("hck,kd->chd", probs_low, value_block).astype(jnp.bfloat16)
        out_wide = lax.optimization_barrier(out_block).astype(jnp.float32)
        delta = jnp.einsum("chd,chd->hc", dout_block, out_wide)
        grad_probs = jnp.einsum("chd,kd->hck", dout_block, value_block)
        grad_logits = (probs_full * (grad_probs - delta[..., None])).astype(jnp.bfloat16)
        grad_logits = lax.optimization_barrier(grad_logits).astype(jnp.float32)
        grad_query = (jnp.einsum("hck,kd->chd", grad_logits, key_block) * scale_factor).astype(jnp.bfloat16)
        key_add = jnp.einsum("hck,chd->kd", grad_logits, query_block)
        value_add = jnp.einsum("hck,chd->kd", probs_low, dout_block)
        grad_keys = lax.dynamic_update_slice_in_dim(grad_keys, lax.dynamic_slice_in_dim(grad_keys, start, span_rows, 0) + key_add, start, 0)
        grad_values = lax.dynamic_update_slice_in_dim(grad_values, lax.dynamic_slice_in_dim(grad_values, start, span_rows, 0) + value_add, start, 0)
        return (grad_keys, grad_values), (out_block, grad_query)

    initial = (jnp.zeros((margin + TOKENS, HEAD_DIM), jnp.float32), jnp.zeros((margin + TOKENS, HEAD_DIM), jnp.float32))
    sums, blocks = lax.scan(visit, initial, jnp.arange(STRETCHES, dtype=jnp.int32))
    out_blocks, query_blocks = blocks
    attention_out = out_blocks[inverse].reshape(TOKENS, H, HEAD_DIM)
    grad_queries = query_blocks[inverse].reshape(TOKENS, H, HEAD_DIM)
    key_sums = sums[0][margin:].reshape(STRETCHES, STRETCH, HEAD_DIM)[inverse].reshape(TOKENS, HEAD_DIM)
    value_sums = sums[1][margin:].reshape(STRETCHES, STRETCH, HEAD_DIM)[inverse].reshape(TOKENS, HEAD_DIM)
    grad_keys = (key_sums * scale_factor).astype(jnp.bfloat16)
    grad_values = value_sums.astype(jnp.bfloat16)
    return (attention_out, grad_queries, grad_keys, grad_values)
```

```python
import functools
import math

import jax
import jax.numpy as jnp
from jax import lax
from jax.experimental import pallas as pl
from jax.experimental.pallas import tpu as pltpu
from jax.sharding import PartitionSpec as P

MAXDOC = 4096
MASKED = -1e30
LOG2E = math.log2(math.e)
TQ = 256
TK = 512


def attention_kernel(
    sizes, first_ref, last_ref, slot_ref, q_ref, do_ref, start_ref, kv_ref, out_ref, dq_ref, dkv_ref, acc_ref
):
    heads, width, rows, tiles, reach, scale = sizes
    step = pl.program_id(0)
    half = step // tiles
    query_stretch = slot_ref[2 * (reach + 1) + half]
    query_first = query_stretch * rows + (step % tiles) * TQ
    lanes = heads * TQ

    @pl.when(step == 0)
    def _():
        def clear(slot, carried):
            acc_ref[slot] = jnp.zeros((rows, 2 * width), jnp.float32)
            return carried

        lax.fori_loop(0, 2 * (reach + 1), clear, 0)

    def heads_first(ref):
        parts = [ref[:, h * width : (h + 1) * width] for h in range(heads)]
        return jnp.concatenate(parts, axis=0) if heads > 1 else parts[0]

    q = heads_first(q_ref)
    do = heads_first(do_ref)
    q_t = q.T
    do_t = do.T
    starts = start_ref[0]
    spread = lax.broadcasted_iota(jnp.int32, (1, lanes), 1) % TQ + query_first - starts
    key_row = lax.broadcasted_iota(jnp.int32, (TK, 1), 0)

    def place(tile):
        stretch = tile * TK // rows
        slot = slot_ref[half * (reach + 1) + query_stretch - stretch]
        return slot, pl.multiple_of(tile * TK - stretch * rows, TK)

    def logits2(tile, key_part):
        s = jnp.dot(key_part, q_t, preferred_element_type=jnp.float32) * (scale * LOG2E)
        behind = (key_row + tile * TK) - starts
        return jnp.where((behind >= 0) & (behind <= spread), s, MASKED)

    def forward(tile, carried):
        top, total, acc = carried
        slot, row = place(tile)
        key_part = kv_ref[slot, pl.ds(row, TK), :width]
        value_part = kv_ref[slot, pl.ds(row, TK), width:]
        s = logits2(tile, key_part)
        new_top = jnp.maximum(top, jnp.max(s, axis=0, keepdims=True))
        p = jnp.exp2(s - new_top)
        shrink = jnp.exp2(top - new_top)
        total = total * shrink + jnp.sum(p, axis=0, keepdims=True)
        acc = acc * shrink + lax.dot_general(
            value_part, p.astype(jnp.bfloat16), (((0,), (0,)), ((), ())), preferred_element_type=jnp.float32
        )
        return new_top, total, acc

    tile_low = first_ref[step] // TK
    tile_high = (query_first + TQ - 1) // TK + 1
    top, total, acc = lax.fori_loop(
        tile_low,
        tile_high,
        forward,
        (
            jnp.full((1, lanes), MASKED, jnp.float32),
            jnp.zeros((1, lanes), jnp.float32),
            jnp.zeros((width, lanes), jnp.float32),
        ),
    )
    out_t = (acc / total).astype(jnp.bfloat16)
    log_total = top + jnp.log2(total)
    delta = jnp.sum(do_t.astype(jnp.float32) * out_t.astype(jnp.float32), axis=0, keepdims=True)
    out = out_t.T
    for h in range(heads):
        out_ref[:, h * width : (h + 1) * width] = out[h * TQ : (h + 1) * TQ]

    def backward(tile, dq_t):
        slot, row = place(tile)
        key_part = kv_ref[slot, pl.ds(row, TK), :width]
        value_part = kv_ref[slot, pl.ds(row, TK), width:]
        p = jnp.exp2(logits2(tile, key_part) - log_total)
        dp = jnp.dot(value_part, do_t, preferred_element_type=jnp.float32)
        ds = (p * (dp - delta)).astype(jnp.bfloat16)
        acc_ref[slot, pl.ds(row, TK), :width] += jnp.dot(ds, q, preferred_element_type=jnp.float32)
        acc_ref[slot, pl.ds(row, TK), width:] += jnp.dot(
            p.astype(jnp.bfloat16), do, preferred_element_type=jnp.float32
        )
        return dq_t + lax.dot_general(
            key_part, ds, (((0,), (0,)), ((), ())), preferred_element_type=jnp.float32
        )

    dq_t = lax.fori_loop(tile_low, tile_high, backward, jnp.zeros((width, lanes), jnp.float32))
    dq = (dq_t * scale).astype(jnp.bfloat16).T
    for h in range(heads):
        dq_ref[:, h * width : (h + 1) * width] = dq[h * TQ : (h + 1) * TQ]

    @pl.when(step == 2 * tiles - 1)
    def _():
        def finish(slot, carried):
            dkv_ref[slot] = acc_ref[slot].astype(jnp.bfloat16)
            return carried

        lax.fori_loop(0, 2 * (reach + 1), finish, 0)


def run_attention(queries, grad_out, window, first, last, slots, starts, rows, reach):
    tok_rows, heads, width = queries.shape
    tiles = rows // TQ
    sizes = (heads, width, rows, tiles, reach, 1.0 / width)
    slot_count = window.shape[0]
    row_spec = pl.BlockSpec((TQ, heads * width), lambda t, *_: (t, 0))
    all_spec = pl.BlockSpec((slot_count, rows, 2 * width), lambda t, *_: (0, 0, 0))
    out, dq, dkv = pl.pallas_call(
        functools.partial(attention_kernel, sizes),
        out_shape=(
            jax.ShapeDtypeStruct((tok_rows, heads * width), jnp.bfloat16),
            jax.ShapeDtypeStruct((tok_rows, heads * width), jnp.bfloat16),
            jax.ShapeDtypeStruct(window.shape, jnp.bfloat16),
        ),
        grid_spec=pltpu.PrefetchScalarGridSpec(
            num_scalar_prefetch=3,
            grid=(2 * tiles,),
            in_specs=[
                row_spec,
                row_spec,
                pl.BlockSpec((1, 1, heads * TQ), lambda t, *_: (t, 0, 0)),
                all_spec,
            ],
            out_specs=(row_spec, row_spec, all_spec),
            scratch_shapes=[pltpu.VMEM((slot_count, rows, 2 * width), jnp.float32)],
        ),
        compiler_params=pltpu.CompilerParams(
            dimension_semantics=("arbitrary",), vmem_limit_bytes=56 * 1024 * 1024
        ),
    )(
        first,
        last,
        slots,
        queries.reshape(tok_rows, heads * width),
        grad_out.reshape(tok_rows, heads * width),
        starts,
        window,
    )
    return out.reshape(queries.shape), dq.reshape(queries.shape), dkv


def extra_pairs(n, k):
    pairs = []
    for below in range(1, k):
        if k < 2 * below + 1 and k >= below + 1 and below < n:
            pairs.append((n - k + below, n - 1 - below))
    return pairs


def per_device(queries, key_vectors, value_vectors, grad_out, doc_lengths):
    n = lax.axis_size("ctx")
    here = lax.axis_index("ctx")
    tok_rows, heads, width = queries.shape
    rows = tok_rows // 2
    reach = (MAXDOC - 1 + rows - 1) // rows
    tiles = rows // TQ
    packed = jnp.concatenate([key_vectors, value_vectors], axis=1)
    low, high = packed[:rows], packed[rows:]

    def move(x, pairs):
        return lax.ppermute(x, "ctx", pairs)

    def up(k):
        return [(i, i + k) for i in range(n - k)]

    def down(k):
        return [(i + k, i) for i in range(n - k)]

    def back(pairs):
        return [(b, a) for a, b in pairs]

    lows = [move(low, up(k)) for k in range(1, reach + 1)]
    highs = []
    for k in range(1, reach + 1):
        part = move(high, down(k))
        pairs = extra_pairs(n, k)
        if pairs:
            part = jnp.where(here >= n - k, move(low, pairs), part)
        highs.append(part)
    window = jnp.stack([low] + lows + [high] + highs)

    steps = jnp.arange(reach + 1, dtype=jnp.int32)
    again = 2 * here - (2 * n - 1) + steps
    slots = jnp.concatenate(
        [
            steps,
            jnp.where((again >= 0) & (again <= reach), again, steps + reach + 1),
            jnp.stack([here, 2 * n - 1 - here]),
        ]
    ).astype(jnp.int32)

    doc_ends = jnp.cumsum(doc_lengths)
    stretch = jnp.stack([here, 2 * n - 1 - here]).astype(jnp.int32)
    pos = (stretch[:, None] * rows + jnp.arange(rows, dtype=jnp.int32)[None, :]).reshape(-1)
    begin = jnp.max(jnp.where(doc_ends[None, :] <= pos[:, None], doc_ends[None, :], 0), axis=1)
    begin = begin.astype(jnp.int32).reshape(2 * tiles, TQ)
    starts = jnp.tile(begin, (1, heads)).reshape(2 * tiles, 1, heads * TQ)
    out, dq, dkv = run_attention(
        queries, grad_out, window, begin[:, 0], begin[:, -1], slots, starts, rows, reach
    )

    low_total = dkv[0].astype(jnp.float32)
    high_total = dkv[reach + 1].astype(jnp.float32)
    for k in range(1, reach + 1):
        low_total = low_total + move(dkv[k], back(up(k))).astype(jnp.float32)
        term = dkv[reach + 1 + k]
        high_total = high_total + move(term, back(down(k))).astype(jnp.float32)
        pairs = extra_pairs(n, k)
        if pairs:
            low_total = low_total + move(term, back(pairs)).astype(jnp.float32)
    total = jnp.concatenate([low_total, high_total], axis=0)
    shares = lax.psum_scatter(total, "head", scatter_dimension=0, tiled=True)
    grad_keys = (shares[:, :width] * (1.0 / width)).astype(jnp.bfloat16)
    grad_values = shares[:, width:].astype(jnp.bfloat16)
    return out, dq, grad_keys, grad_values


def solution(mesh):
    placed = (P("ctx", "head", None), P("ctx", None), P("ctx", None), P("ctx", "head", None), P())
    return jax.shard_map(
        per_device,
        mesh=mesh,
        in_specs=placed,
        out_specs=(
            P("ctx", "head", None),
            P("ctx", "head", None),
            P(("ctx", "head"), None),
            P(("ctx", "head"), None),
        ),
        check_vma=False,
    )
```

```python
import functools
import math

import jax
import jax.numpy as jnp
from jax import lax
from jax.experimental import pallas as pl
from jax.experimental.pallas import tpu as pltpu
from jax.sharding import PartitionSpec as P

MAXDOC = 4096
MASKED = -1e30
LOG2E = math.log2(math.e)
TQ = 256
TK = 512


def attention_kernel(
    sizes, first_ref, last_ref, slot_ref, q_ref, do_ref, start_ref, kv_ref, out_ref, dq_ref, dkv_ref, acc_ref
):
    heads, width, rows, tiles, reach, scale = sizes
    step = pl.program_id(0)
    half = step // tiles
    query_stretch = slot_ref[2 * (reach + 1) + half]
    query_first = query_stretch * rows + (step % tiles) * TQ
    lanes = heads * TQ

    @pl.when(step == 0)
    def _():
        def clear(slot, carried):
            acc_ref[slot] = jnp.zeros((rows, 2 * width), jnp.float32)
            return carried

        lax.fori_loop(0, 2 * (reach + 1), clear, 0)

    def heads_first(ref):
        parts = [ref[:, h * width : (h + 1) * width] for h in range(heads)]
        return jnp.concatenate(parts, axis=0) if heads > 1 else parts[0]

    q = heads_first(q_ref)
    do = heads_first(do_ref)
    q_t = q.T
    do_t = do.T
    starts = start_ref[0]
    spread = lax.broadcasted_iota(jnp.int32, (1, lanes), 1) % TQ + query_first - starts
    key_row = lax.broadcasted_iota(jnp.int32, (TK, 1), 0)

    def place(tile):
        stretch = tile * TK // rows
        slot = slot_ref[half * (reach + 1) + query_stretch - stretch]
        return slot, pl.multiple_of(tile * TK - stretch * rows, TK)

    def logits2(tile, key_part):
        s = jnp.dot(key_part, q_t, preferred_element_type=jnp.float32) * (scale * LOG2E)
        behind = (key_row + tile * TK) - starts
        return jnp.where((behind >= 0) & (behind <= spread), s, MASKED)

    def forward(tile, carried):
        top, total, acc = carried
        slot, row = place(tile)
        key_part = kv_ref[slot, pl.ds(row, TK), :width]
        value_part = kv_ref[slot, pl.ds(row, TK), width:]
        s = logits2(tile, key_part)
        new_top = jnp.maximum(top, jnp.max(s, axis=0, keepdims=True))
        p = jnp.exp2(s - new_top)
        shrink = jnp.exp2(top - new_top)
        total = total * shrink + jnp.sum(p, axis=0, keepdims=True)
        acc = acc * shrink + lax.dot_general(
            value_part, p.astype(jnp.bfloat16), (((0,), (0,)), ((), ())), preferred_element_type=jnp.float32
        )
        return new_top, total, acc

    tile_low = first_ref[step] // TK
    tile_high = (query_first + TQ - 1) // TK + 1
    top, total, acc = lax.fori_loop(
        tile_low,
        tile_high,
        forward,
        (
            jnp.full((1, lanes), MASKED, jnp.float32),
            jnp.zeros((1, lanes), jnp.float32),
            jnp.zeros((width, lanes), jnp.float32),
        ),
    )
    out_t = (acc / total).astype(jnp.bfloat16)
    log_total = top + jnp.log2(total)
    delta = jnp.sum(do_t.astype(jnp.float32) * out_t.astype(jnp.float32), axis=0, keepdims=True)
    out = out_t.T
    for h in range(heads):
        out_ref[:, h * width : (h + 1) * width] = out[h * TQ : (h + 1) * TQ]

    def backward(tile, dq_t):
        slot, row = place(tile)
        key_part = kv_ref[slot, pl.ds(row, TK), :width]
        value_part = kv_ref[slot, pl.ds(row, TK), width:]
        p = jnp.exp2(logits2(tile, key_part) - log_total)
        dp = jnp.dot(value_part, do_t, preferred_element_type=jnp.float32)
        ds = (p * (dp - delta)).astype(jnp.bfloat16)
        acc_ref[slot, pl.ds(row, TK), :width] += jnp.dot(ds, q, preferred_element_type=jnp.float32)
        acc_ref[slot, pl.ds(row, TK), width:] += jnp.dot(
            p.astype(jnp.bfloat16), do, preferred_element_type=jnp.float32
        )
        return dq_t + lax.dot_general(
            key_part, ds, (((0,), (0,)), ((), ())), preferred_element_type=jnp.float32
        )

    dq_t = lax.fori_loop(tile_low, tile_high, backward, jnp.zeros((width, lanes), jnp.float32))
    dq = (dq_t * scale).astype(jnp.bfloat16).T
    for h in range(heads):
        dq_ref[:, h * width : (h + 1) * width] = dq[h * TQ : (h + 1) * TQ]

    @pl.when(step == 2 * tiles - 1)
    def _():
        def finish(slot, carried):
            dkv_ref[slot] = acc_ref[slot].astype(jnp.bfloat16)
            return carried

        lax.fori_loop(0, 2 * (reach + 1), finish, 0)


def run_attention(queries, grad_out, window, first, last, slots, starts, rows, reach):
    tok_rows, heads, width = queries.shape
    tiles = rows // TQ
    sizes = (heads, width, rows, tiles, reach, 1.0 / width)
    slot_count = window.shape[0]
    row_spec = pl.BlockSpec((TQ, heads * width), lambda t, *_: (t, 0))
    all_spec = pl.BlockSpec((slot_count, rows, 2 * width), lambda t, *_: (0, 0, 0))
    out, dq, dkv = pl.pallas_call(
        functools.partial(attention_kernel, sizes),
        out_shape=(
            jax.ShapeDtypeStruct((tok_rows, heads * width), jnp.bfloat16),
            jax.ShapeDtypeStruct((tok_rows, heads * width), jnp.bfloat16),
            jax.ShapeDtypeStruct(window.shape, jnp.bfloat16),
        ),
        grid_spec=pltpu.PrefetchScalarGridSpec(
            num_scalar_prefetch=3,
            grid=(2 * tiles,),
            in_specs=[
                row_spec,
                row_spec,
                pl.BlockSpec((1, 1, heads * TQ), lambda t, *_: (t, 0, 0)),
                all_spec,
            ],
            out_specs=(row_spec, row_spec, all_spec),
            scratch_shapes=[pltpu.VMEM((slot_count, rows, 2 * width), jnp.float32)],
        ),
        compiler_params=pltpu.CompilerParams(
            dimension_semantics=("arbitrary",), vmem_limit_bytes=56 * 1024 * 1024
        ),
    )(
        first,
        last,
        slots,
        queries.reshape(tok_rows, heads * width),
        grad_out.reshape(tok_rows, heads * width),
        starts,
        window,
    )
    return out.reshape(queries.shape), dq.reshape(queries.shape), dkv


def extra_pairs(n, k):
    pairs = []
    for below in range(1, k):
        if k < 2 * below + 1 and k >= below + 1 and below < n:
            pairs.append((n - k + below, n - 1 - below))
    return pairs


def gather_kernel(n, reach, x_ref, window_ref, send_sem, extra_sem, pass_sem, recv_sem, local_sem):
    here = lax.axis_index("ctx")
    core = here % 2
    sibling = here + 1 - 2 * core
    rows = window_ref.shape[1]
    part_rows = rows // 2

    barrier = pltpu.get_barrier_semaphore()
    for by in range(1, n):
        pl.semaphore_signal(
            barrier, inc=1, device_id={"ctx": (here + by) % n}, device_id_type=pl.DeviceIdType.MESH
        )
    pl.semaphore_wait(barrier, n - 1)

    def slot_of(f, k):
        return f * (reach + 1) + k

    def own(f, p):
        return x_ref.at[pl.ds(f * rows + p * part_rows, part_rows)]

    def into(f, k, p):
        return window_ref.at[slot_of(f, k), pl.ds(p * part_rows, part_rows)]

    def copy(src, f, k, p, sem, device):
        return pltpu.make_async_remote_copy(
            src_ref=src,
            dst_ref=into(f, k, p),
            send_sem=sem,
            recv_sem=recv_sem.at[slot_of(f, k), p],
            device_id={"ctx": device},
            device_id_type=pl.DeviceIdType.MESH,
        )

    locals_ = [
        pltpu.make_async_copy(
            x_ref.at[pl.ds(f * rows, rows)], window_ref.at[slot_of(f, 0)], local_sem.at[f]
        )
        for f in range(2)
    ]
    for c in locals_:
        c.start()

    def near(f, device_core):
        return device_core == f

    direct = []
    for k in range(reach, 0, -1):
        for f in range(2):
            target = here + k if f == 0 else here - k
            valid = target < n if f == 0 else target >= 0
            target_near = near(f, (core + k) % 2)
            for p in range(2):
                sent = jnp.where(
                    target_near, p == 0 or k == reach, p == 1 or k == 1
                )
                direct.append((valid & sent, copy(own(f, p), f, k, p, send_sem.at[slot_of(f, k), p], target)))
        for source, target in extra_pairs(n, k):
            for p in range(2):
                is_near = target % 2 == 1
                if (is_near and (p == 0 or k == reach)) or (not is_near and (p == 1 or source == target + 1)):
                    direct.append(
                        (here == source, copy(own(0, p), 1, k, p, extra_sem.at[k - 1, target % 2, p], target))
                    )
    for when, c in direct:
        pl.when(when)(c.start)

    def has(f, k):
        if f == 0:
            return here - k >= 0
        found = here + k < n
        for source, target in extra_pairs(n, k):
            found = found | (here == target)
        return found

    passed = []
    arrivals = []
    for k in range(1, reach + 1):
        for f in range(2):
            present = has(f, k)
            here_near = near(f, core)
            whole = jnp.where(here_near, k == reach, k == 1)
            for source, target in extra_pairs(n, k) if f == 1 else []:
                if source == target + 1 and target % 2 == 0:
                    whole = whole | (here == target)
            for p in range(2):
                from_source = whole | (here_near == (p == 0))
                next_k = k + 1 if p == 0 else k - 1
                forwards = 1 <= next_k <= reach
                if forwards:
                    c = copy(into(f, k, p), f, next_k, p, pass_sem.at[slot_of(f, k)], sibling)
                    when = present & (here_near == (p == 0)) & jnp.logical_not(whole)
                    arrived = copy(into(f, k, p), f, k, p, pass_sem.at[slot_of(f, k)], sibling)
                    passed.append((when, c, arrived))
                    arrivals.append((present & jnp.logical_not(when), arrived))
                else:
                    arrived = copy(into(f, k, p), f, k, p, pass_sem.at[slot_of(f, k)], sibling)
                    arrivals.append((present, arrived))
    for when, c, arrived in passed:

        @pl.when(when)
        def _():
            arrived.wait_recv()
            c.start()

    for when, arrived in arrivals:
        pl.when(when)(arrived.wait_recv)
    for when, c in direct:
        pl.when(when)(c.wait_send)
    for when, c, arrived in passed:
        pl.when(when)(c.wait_send)
    for c in locals_:
        c.wait()


def gather(packed, n, reach):
    rows, columns = packed.shape[0] // 2, packed.shape[1]
    slots = 2 * (reach + 1)
    return pl.pallas_call(
        functools.partial(gather_kernel, n, reach),
        out_shape=jax.ShapeDtypeStruct((slots, rows, columns), packed.dtype),
        in_specs=[pl.BlockSpec(memory_space=pl.ANY)],
        out_specs=pl.BlockSpec(memory_space=pl.ANY),
        scratch_shapes=[
            pltpu.SemaphoreType.DMA((slots, 2)),
            pltpu.SemaphoreType.DMA((reach, 2, 2)),
            pltpu.SemaphoreType.DMA((slots,)),
            pltpu.SemaphoreType.DMA((slots, 2)),
            pltpu.SemaphoreType.DMA((2,)),
        ],
        compiler_params=pltpu.CompilerParams(collective_id=0, has_side_effects=True),
    )(packed)


def per_device(queries, key_vectors, value_vectors, grad_out, doc_lengths):
    n = lax.axis_size("ctx")
    here = lax.axis_index("ctx")
    tok_rows, heads, width = queries.shape
    rows = tok_rows // 2
    reach = (MAXDOC - 1 + rows - 1) // rows
    tiles = rows // TQ
    packed = jnp.concatenate([key_vectors, value_vectors], axis=1)

    def move(x, pairs):
        return lax.ppermute(x, "ctx", pairs)

    def up(k):
        return [(i, i + k) for i in range(n - k)]

    def down(k):
        return [(i + k, i) for i in range(n - k)]

    def back(pairs):
        return [(b, a) for a, b in pairs]

    window = gather(packed, n, reach)

    steps = jnp.arange(reach + 1, dtype=jnp.int32)
    again = 2 * here - (2 * n - 1) + steps
    slots = jnp.concatenate(
        [
            steps,
            jnp.where((again >= 0) & (again <= reach), again, steps + reach + 1),
            jnp.stack([here, 2 * n - 1 - here]),
        ]
    ).astype(jnp.int32)

    doc_ends = jnp.cumsum(doc_lengths)
    stretch = jnp.stack([here, 2 * n - 1 - here]).astype(jnp.int32)
    pos = (stretch[:, None] * rows + jnp.arange(rows, dtype=jnp.int32)[None, :]).reshape(-1)
    begin = jnp.max(jnp.where(doc_ends[None, :] <= pos[:, None], doc_ends[None, :], 0), axis=1)
    begin = begin.astype(jnp.int32).reshape(2 * tiles, TQ)
    starts = jnp.tile(begin, (1, heads)).reshape(2 * tiles, 1, heads * TQ)
    out, dq, dkv = run_attention(
        queries, grad_out, window, begin[:, 0], begin[:, -1], slots, starts, rows, reach
    )

    low_total = dkv[0].astype(jnp.float32)
    high_total = dkv[reach + 1].astype(jnp.float32)
    for k in range(1, reach + 1):
        low_total = low_total + move(dkv[k], back(up(k))).astype(jnp.float32)
        term = dkv[reach + 1 + k]
        high_total = high_total + move(term, back(down(k))).astype(jnp.float32)
        pairs = extra_pairs(n, k)
        if pairs:
            low_total = low_total + move(term, back(pairs)).astype(jnp.float32)
    total = jnp.concatenate([low_total, high_total], axis=0).astype(jnp.bfloat16)
    shares = lax.psum_scatter(total, "head", scatter_dimension=0, tiled=True)
    grad_keys = (shares[:, :width].astype(jnp.float32) * (1.0 / width)).astype(jnp.bfloat16)
    grad_values = shares[:, width:].astype(jnp.bfloat16)
    return out, dq, grad_keys, grad_values


def solution(mesh):
    placed = (P("ctx", "head", None), P("ctx", None), P("ctx", None), P("ctx", "head", None), P())
    return jax.shard_map(
        per_device,
        mesh=mesh,
        in_specs=placed,
        out_specs=(
            P("ctx", "head", None),
            P("ctx", "head", None),
            P(("ctx", "head"), None),
            P(("ctx", "head"), None),
        ),
        check_vma=False,
    )
```

```python
import functools
import math

import jax
import jax.numpy as jnp
from jax import lax
from jax.experimental import pallas as pl
from jax.experimental.pallas import tpu as pltpu
from jax.sharding import PartitionSpec as P

MAXDOC = 4096
MASKED = -1e30
LOG2E = math.log2(math.e)
TQ = 256
TK = 512


def attention_kernel(
    sizes, first_ref, last_ref, slot_ref, q_ref, do_ref, start_ref, kv_ref, out_ref, dq_ref, dkv_ref, acc_ref
):
    heads, width, rows, tiles, reach, scale = sizes
    step = pl.program_id(0)
    half = step // tiles
    query_stretch = slot_ref[2 * (reach + 1) + half]
    query_first = query_stretch * rows + (step % tiles) * TQ
    lanes = heads * TQ

    @pl.when(step == 0)
    def _():
        def clear(slot, carried):
            acc_ref[slot] = jnp.zeros((rows, 2 * width), jnp.float32)
            return carried

        lax.fori_loop(0, 2 * (reach + 1), clear, 0)

    def heads_first(ref):
        parts = [ref[:, h * width : (h + 1) * width] for h in range(heads)]
        return jnp.concatenate(parts, axis=0) if heads > 1 else parts[0]

    q = heads_first(q_ref)
    do = heads_first(do_ref)
    q_t = q.T
    do_t = do.T
    starts = start_ref[0]
    spread = lax.broadcasted_iota(jnp.int32, (1, lanes), 1) % TQ + query_first - starts
    key_row = lax.broadcasted_iota(jnp.int32, (TK, 1), 0)

    def place(tile):
        stretch = tile * TK // rows
        slot = slot_ref[half * (reach + 1) + query_stretch - stretch]
        return slot, pl.multiple_of(tile * TK - stretch * rows, TK)

    def logits2(tile, key_part):
        s = jnp.dot(key_part, q_t, preferred_element_type=jnp.float32) * (scale * LOG2E)
        behind = (key_row + tile * TK) - starts
        return jnp.where((behind >= 0) & (behind <= spread), s, MASKED)

    def forward(tile, carried):
        top, total, acc = carried
        slot, row = place(tile)
        key_part = kv_ref[slot, pl.ds(row, TK), :width]
        value_part = kv_ref[slot, pl.ds(row, TK), width:]
        s = logits2(tile, key_part)
        new_top = jnp.maximum(top, jnp.max(s, axis=0, keepdims=True))
        p = jnp.exp2(s - new_top)
        shrink = jnp.exp2(top - new_top)
        total = total * shrink + jnp.sum(p, axis=0, keepdims=True)
        acc = acc * shrink + lax.dot_general(
            value_part, p.astype(jnp.bfloat16), (((0,), (0,)), ((), ())), preferred_element_type=jnp.float32
        )
        return new_top, total, acc

    tile_low = first_ref[step] // TK
    tile_high = (query_first + TQ - 1) // TK + 1
    top, total, acc = lax.fori_loop(
        tile_low,
        tile_high,
        forward,
        (
            jnp.full((1, lanes), MASKED, jnp.float32),
            jnp.zeros((1, lanes), jnp.float32),
            jnp.zeros((width, lanes), jnp.float32),
        ),
    )
    out_t = (acc / total).astype(jnp.bfloat16)
    log_total = top + jnp.log2(total)
    delta = jnp.sum(do_t.astype(jnp.float32) * out_t.astype(jnp.float32), axis=0, keepdims=True)
    out = out_t.T
    for h in range(heads):
        out_ref[:, h * width : (h + 1) * width] = out[h * TQ : (h + 1) * TQ]

    def backward(tile, dq_t):
        slot, row = place(tile)
        key_part = kv_ref[slot, pl.ds(row, TK), :width]
        value_part = kv_ref[slot, pl.ds(row, TK), width:]
        p = jnp.exp2(logits2(tile, key_part) - log_total)
        dp = jnp.dot(value_part, do_t, preferred_element_type=jnp.float32)
        ds = (p * (dp - delta)).astype(jnp.bfloat16)
        acc_ref[slot, pl.ds(row, TK), :width] += jnp.dot(ds, q, preferred_element_type=jnp.float32)
        acc_ref[slot, pl.ds(row, TK), width:] += jnp.dot(
            p.astype(jnp.bfloat16), do, preferred_element_type=jnp.float32
        )
        return dq_t + lax.dot_general(
            key_part, ds, (((0,), (0,)), ((), ())), preferred_element_type=jnp.float32
        )

    dq_t = lax.fori_loop(tile_low, tile_high, backward, jnp.zeros((width, lanes), jnp.float32))
    dq = (dq_t * scale).astype(jnp.bfloat16).T
    for h in range(heads):
        dq_ref[:, h * width : (h + 1) * width] = dq[h * TQ : (h + 1) * TQ]

    @pl.when(step == 2 * tiles - 1)
    def _():
        def finish(slot, carried):
            dkv_ref[slot] = acc_ref[slot].astype(jnp.bfloat16)
            return carried

        lax.fori_loop(0, 2 * (reach + 1), finish, 0)


def run_attention(queries, grad_out, window, first, last, slots, starts, rows, reach):
    tok_rows, heads, width = queries.shape
    tiles = rows // TQ
    sizes = (heads, width, rows, tiles, reach, 1.0 / width)
    slot_count = window.shape[0]
    row_spec = pl.BlockSpec((TQ, heads * width), lambda t, *_: (t, 0))
    all_spec = pl.BlockSpec((slot_count, rows, 2 * width), lambda t, *_: (0, 0, 0))
    out, dq, dkv = pl.pallas_call(
        functools.partial(attention_kernel, sizes),
        out_shape=(
            jax.ShapeDtypeStruct((tok_rows, heads * width), jnp.bfloat16),
            jax.ShapeDtypeStruct((tok_rows, heads * width), jnp.bfloat16),
            jax.ShapeDtypeStruct(window.shape, jnp.bfloat16),
        ),
        grid_spec=pltpu.PrefetchScalarGridSpec(
            num_scalar_prefetch=3,
            grid=(2 * tiles,),
            in_specs=[
                row_spec,
                row_spec,
                pl.BlockSpec((1, 1, heads * TQ), lambda t, *_: (t, 0, 0)),
                all_spec,
            ],
            out_specs=(row_spec, row_spec, all_spec),
            scratch_shapes=[pltpu.VMEM((slot_count, rows, 2 * width), jnp.float32)],
        ),
        compiler_params=pltpu.CompilerParams(
            dimension_semantics=("arbitrary",), vmem_limit_bytes=56 * 1024 * 1024
        ),
    )(
        first,
        last,
        slots,
        queries.reshape(tok_rows, heads * width),
        grad_out.reshape(tok_rows, heads * width),
        starts,
        window,
    )
    return out.reshape(queries.shape), dq.reshape(queries.shape), dkv


def extra_pairs(n, k):
    pairs = []
    for below in range(1, k):
        if k < 2 * below + 1 and k >= below + 1 and below < n:
            pairs.append((n - k + below, n - 1 - below))
    return pairs


def gather_kernel(n, reach, x_ref, window_ref, send_sem, extra_sem, pass_sem, recv_sem, local_sem):
    here = lax.axis_index("ctx")
    core = here % 2
    sibling = here + 1 - 2 * core
    rows = window_ref.shape[1]
    part_rows = rows // 2

    barrier = pltpu.get_barrier_semaphore()
    for by in range(1, n):
        pl.semaphore_signal(
            barrier, inc=1, device_id={"ctx": (here + by) % n}, device_id_type=pl.DeviceIdType.MESH
        )
    pl.semaphore_wait(barrier, n - 1)

    def slot_of(f, k):
        return f * (reach + 1) + k

    def own(f, p):
        return x_ref.at[pl.ds(f * rows + p * part_rows, part_rows)]

    def into(f, k, p):
        return window_ref.at[slot_of(f, k), pl.ds(p * part_rows, part_rows)]

    def copy(src, f, k, p, sem, device):
        return pltpu.make_async_remote_copy(
            src_ref=src,
            dst_ref=into(f, k, p),
            send_sem=sem,
            recv_sem=recv_sem.at[slot_of(f, k), p],
            device_id={"ctx": device},
            device_id_type=pl.DeviceIdType.MESH,
        )

    locals_ = [
        pltpu.make_async_copy(
            x_ref.at[pl.ds(f * rows, rows)], window_ref.at[slot_of(f, 0)], local_sem.at[f]
        )
        for f in range(2)
    ]
    for c in locals_:
        c.start()

    def near(f, device_core):
        return device_core == f

    direct = []
    for k in range(reach, 0, -1):
        for f in range(2):
            target = here + k if f == 0 else here - k
            valid = target < n if f == 0 else target >= 0
            target_near = near(f, (core + k) % 2)
            for p in range(2):
                sent = jnp.where(
                    target_near, p == 0 or k == reach, p == 1 or k == 1
                )
                direct.append((valid & sent, copy(own(f, p), f, k, p, send_sem.at[slot_of(f, k), p], target)))
        for source, target in extra_pairs(n, k):
            for p in range(2):
                is_near = target % 2 == 1
                if (is_near and (p == 0 or k == reach)) or (not is_near and (p == 1 or source == target + 1)):
                    direct.append(
                        (here == source, copy(own(0, p), 1, k, p, extra_sem.at[k - 1, target % 2, p], target))
                    )
    for when, c in direct:
        pl.when(when)(c.start)

    def has(f, k):
        if f == 0:
            return here - k >= 0
        found = here + k < n
        for source, target in extra_pairs(n, k):
            found = found | (here == target)
        return found

    passed = []
    arrivals = []
    for k in range(1, reach + 1):
        for f in range(2):
            present = has(f, k)
            here_near = near(f, core)
            whole = jnp.where(here_near, k == reach, k == 1)
            for source, target in extra_pairs(n, k) if f == 1 else []:
                if source == target + 1 and target % 2 == 0:
                    whole = whole | (here == target)
            for p in range(2):
                from_source = whole | (here_near == (p == 0))
                next_k = k + 1 if p == 0 else k - 1
                forwards = 1 <= next_k <= reach
                if forwards:
                    c = copy(into(f, k, p), f, next_k, p, pass_sem.at[slot_of(f, k)], sibling)
                    when = present & (here_near == (p == 0)) & jnp.logical_not(whole)
                    arrived = copy(into(f, k, p), f, k, p, pass_sem.at[slot_of(f, k)], sibling)
                    passed.append((when, c, arrived))
                    arrivals.append((present & jnp.logical_not(when), arrived))
                else:
                    arrived = copy(into(f, k, p), f, k, p, pass_sem.at[slot_of(f, k)], sibling)
                    arrivals.append((present, arrived))
    for when, c, arrived in passed:

        @pl.when(when)
        def _():
            arrived.wait_recv()
            c.start()

    for when, arrived in arrivals:
        pl.when(when)(arrived.wait_recv)
    for when, c in direct:
        pl.when(when)(c.wait_send)
    for when, c, arrived in passed:
        pl.when(when)(c.wait_send)
    for c in locals_:
        c.wait()


def gather(packed, n, reach):
    rows, columns = packed.shape[0] // 2, packed.shape[1]
    slots = 2 * (reach + 1)
    return pl.pallas_call(
        functools.partial(gather_kernel, n, reach),
        out_shape=jax.ShapeDtypeStruct((slots, rows, columns), packed.dtype),
        in_specs=[pl.BlockSpec(memory_space=pl.ANY)],
        out_specs=pl.BlockSpec(memory_space=pl.ANY),
        scratch_shapes=[
            pltpu.SemaphoreType.DMA((slots, 2)),
            pltpu.SemaphoreType.DMA((reach, 2, 2)),
            pltpu.SemaphoreType.DMA((slots,)),
            pltpu.SemaphoreType.DMA((slots, 2)),
            pltpu.SemaphoreType.DMA((2,)),
        ],
        compiler_params=pltpu.CompilerParams(collective_id=0, has_side_effects=True),
    )(packed)


def give_back_kernel(
    n, heads, reach, term_ref, key_ref, value_ref,
    land, extra_land, raw_land, mixed, total, outgoing, head_land,
    send_sem, recv_sem, extra_sem, raw_send, raw_recv, head_send, head_recv,
):
    here = lax.axis_index("ctx")
    mine = lax.axis_index("head")
    core = here % 2
    sibling = here + 1 - 2 * core
    rows, columns = term_ref.shape[1], term_ref.shape[2]
    part_rows = rows // 2
    width = columns // 2
    share = 2 * rows // heads

    barrier = pltpu.get_barrier_semaphore()
    for by in range(1, n):
        pl.semaphore_signal(
            barrier, inc=1, device_id={"ctx": (here + by) % n}, device_id_type=pl.DeviceIdType.MESH
        )
    for by in range(1, heads):
        pl.semaphore_signal(
            barrier, inc=1, device_id={"head": (mine + by) % heads}, device_id_type=pl.DeviceIdType.MESH
        )
    pl.semaphore_wait(barrier, n + heads - 2)

    def slot_of(f, k):
        return f * (reach + 1) + k

    def part(p):
        return pl.ds(p * part_rows, part_rows)

    def remote(src, dst, sem, arrival, device):
        return pltpu.make_async_remote_copy(
            src_ref=src, dst_ref=dst, send_sem=sem, recv_sem=arrival,
            device_id={"ctx": device}, device_id_type=pl.DeviceIdType.MESH,
        )

    extras = [(k, a, b) for k in range(1, reach + 1) for a, b in extra_pairs(n, k)]
    raws, straight, mixes = [], [], []
    for k in range(reach, 0, -1):
        for f in range(2):
            slot = slot_of(f, k)
            plain = here - k >= 0 if f == 0 else here + k < n
            back = here - k if f == 0 else here + k
            here_near = core == f
            whole = jnp.where(here_near, k == reach, k == 1)
            routes = [(plain, back, None)]
            present = plain
            for number, (ek, a, b) in enumerate(extras):
                if f == 1 and ek == k:
                    routes.append((here == b, a, number))
                    present = present | (here == b)
                    if a == b + 1 and b % 2 == 0:
                        whole = whole | (here == b)
            shared = present & jnp.logical_not(whole)
            for p in range(2):
                combines = here_near == (p == 0)
                next_k = k - 1 if p == 0 else k + 1
                if 1 <= next_k <= reach:
                    raws.append((
                        shared & jnp.logical_not(combines),
                        remote(
                            term_ref.at[slot, part(p)], raw_land.at[slot_of(f, next_k)],
                            raw_send.at[slot], raw_recv.at[slot_of(f, next_k)], sibling,
                        ),
                    ))
                if 1 <= (k + 1 if p == 0 else k - 1) <= reach:
                    sends = []
                    for when, device, number in routes:
                        dst = land.at[slot, part(p)] if number is None else extra_land.at[number, part(p)]
                        arrival = recv_sem.at[slot, p] if number is None else extra_sem.at[number, p]
                        sends.append((
                            when & shared & combines,
                            remote(mixed.at[slot], dst, send_sem.at[slot, p], arrival, device),
                        ))
                    wait = remote(mixed.at[slot], raw_land.at[slot], raw_send.at[slot], raw_recv.at[slot], sibling)
                    mixes.append((shared & combines, slot, p, wait, sends))
                for when, device, number in routes:
                    dst = land.at[slot, part(p)] if number is None else extra_land.at[number, part(p)]
                    arrival = recv_sem.at[slot, p] if number is None else extra_sem.at[number, p]
                    straight.append((
                        when & whole,
                        remote(term_ref.at[slot, part(p)], dst, send_sem.at[slot, p], arrival, device),
                    ))
    for when, c in raws + straight:
        pl.when(when)(c.start)
    for f in range(2):
        total[pl.ds(f * rows, rows)] = term_ref[slot_of(f, 0)].astype(jnp.float32)
    for when, slot, p, wait, sends in mixes:

        @pl.when(when)
        def _():
            wait.wait_recv()
            mixed[slot] = (
                term_ref[slot, part(p)].astype(jnp.float32) + raw_land[slot].astype(jnp.float32)
            ).astype(jnp.bfloat16)

        for sent, c in sends:
            pl.when(sent)(c.start)

    def add(when, row, buffer, arrival):
        @pl.when(when)
        def _():
            remote(buffer, buffer, raw_send.at[0], arrival, sibling).wait_recv()
            total[pl.ds(row, part_rows)] += buffer[...].astype(jnp.float32)

    for k in range(1, reach + 1):
        for f in range(2):
            target = here + k if f == 0 else here - k
            valid = target < n if f == 0 else target >= 0
            target_near = (core + k) % 2 == f
            for p in range(2):
                sent = jnp.where(target_near, p == 0 or k == reach, p == 1 or k == 1)
                slot = slot_of(f, k)
                add(valid & sent, f * rows + p * part_rows, land.at[slot, part(p)], recv_sem.at[slot, p])
    for number, (k, a, b) in enumerate(extras):
        for p in range(2):
            if b % 2 == 1:
                sent = p == 0 or k == reach
            else:
                sent = p == 1 or a == b + 1
            if sent:
                add(here == a, p * part_rows, extra_land.at[number, part(p)], extra_sem.at[number, p])

    outgoing[...] = total[...].astype(jnp.bfloat16)
    head_copies = []
    for by in range(1, heads):
        other = (mine + by) % heads
        c = pltpu.make_async_remote_copy(
            src_ref=outgoing.at[pl.ds(pl.multiple_of(other * share, share), share)],
            dst_ref=head_land.at[by - 1],
            send_sem=head_send.at[by - 1],
            recv_sem=head_recv.at[by - 1],
            device_id={"head": other},
            device_id_type=pl.DeviceIdType.MESH,
        )
        c.start()
        head_copies.append(c)
    result = total[pl.ds(pl.multiple_of(mine * share, share), share)]
    for by, c in enumerate(head_copies):
        c.wait_recv()
        result = result + head_land[by].astype(jnp.float32)
    key_ref[...] = (result[:, :width] * (1.0 / width)).astype(jnp.bfloat16)
    value_ref[...] = result[:, width:].astype(jnp.bfloat16)
    for when, c in raws + straight:
        pl.when(when)(c.wait_send)
    for when, slot, p, wait, sends in mixes:
        for sent, c in sends:
            pl.when(sent)(c.wait_send)
    for c in head_copies:
        c.wait_send()


def give_back(terms, n, heads, reach):
    slots, rows, columns = terms.shape
    share = 2 * rows // heads
    extras = max(1, sum(len(extra_pairs(n, k)) for k in range(1, reach + 1)))
    low = jnp.bfloat16
    sem = pltpu.SemaphoreType.DMA
    result = jax.ShapeDtypeStruct((share, columns // 2), low)
    return pl.pallas_call(
        functools.partial(give_back_kernel, n, heads, reach),
        out_shape=(result, result),
        in_specs=[pl.BlockSpec(memory_space=pltpu.VMEM)],
        out_specs=(pl.BlockSpec(memory_space=pltpu.VMEM),) * 2,
        scratch_shapes=[
            pltpu.VMEM((slots, rows, columns), low),
            pltpu.VMEM((extras, rows, columns), low),
            pltpu.VMEM((slots, rows // 2, columns), low),
            pltpu.VMEM((slots, rows // 2, columns), low),
            pltpu.VMEM((2 * rows, columns), jnp.float32),
            pltpu.VMEM((2 * rows, columns), low),
            pltpu.VMEM((heads - 1, share, columns), low),
            sem((slots, 2)),
            sem((slots, 2)),
            sem((extras, 2)),
            sem((slots,)),
            sem((slots,)),
            sem((heads - 1,)),
            sem((heads - 1,)),
        ],
        compiler_params=pltpu.CompilerParams(
            collective_id=1, has_side_effects=True, vmem_limit_bytes=50 * 1024 * 1024
        ),
    )(terms)


def per_device(queries, key_vectors, value_vectors, grad_out, doc_lengths):
    n = lax.axis_size("ctx")
    here = lax.axis_index("ctx")
    tok_rows, heads, width = queries.shape
    rows = tok_rows // 2
    reach = (MAXDOC - 1 + rows - 1) // rows
    tiles = rows // TQ
    packed = jnp.concatenate([key_vectors, value_vectors], axis=1)

    window = gather(packed, n, reach)

    steps = jnp.arange(reach + 1, dtype=jnp.int32)
    again = 2 * here - (2 * n - 1) + steps
    slots = jnp.concatenate(
        [
            steps,
            jnp.where((again >= 0) & (again <= reach), again, steps + reach + 1),
            jnp.stack([here, 2 * n - 1 - here]),
        ]
    ).astype(jnp.int32)

    doc_ends = jnp.cumsum(doc_lengths)
    stretch = jnp.stack([here, 2 * n - 1 - here]).astype(jnp.int32)
    pos = (stretch[:, None] * rows + jnp.arange(rows, dtype=jnp.int32)[None, :]).reshape(-1)
    begin = jnp.max(jnp.where(doc_ends[None, :] <= pos[:, None], doc_ends[None, :], 0), axis=1)
    begin = begin.astype(jnp.int32).reshape(2 * tiles, TQ)
    starts = jnp.tile(begin, (1, heads)).reshape(2 * tiles, 1, heads * TQ)
    out, dq, dkv = run_attention(
        queries, grad_out, window, begin[:, 0], begin[:, -1], slots, starts, rows, reach
    )

    grad_keys, grad_values = give_back(dkv, n, lax.axis_size("head"), reach)
    return out, dq, grad_keys, grad_values


def solution(mesh):
    placed = (P("ctx", "head", None), P("ctx", None), P("ctx", None), P("ctx", "head", None), P())
    return jax.shard_map(
        per_device,
        mesh=mesh,
        in_specs=placed,
        out_specs=(
            P("ctx", "head", None),
            P("ctx", "head", None),
            P(("ctx", "head"), None),
            P(("ctx", "head"), None),
        ),
        check_vma=False,
    )
```

```python
import functools
import math

import jax
import jax.numpy as jnp
from jax import lax
from jax.experimental import pallas as pl
from jax.experimental.pallas import tpu as pltpu
from jax.sharding import PartitionSpec as P

MAXDOC = 4096
MASKED = -1e30
LOG2E = math.log2(math.e)
TQ = 256
TK = 512


def attention_kernel(
    sizes, first_ref, last_ref, slot_ref, q_ref, do_ref, start_ref, kv_ref, out_ref, dq_ref, dkv_ref, acc_ref, held_ref
):
    heads, width, rows, tiles, reach, scale = sizes
    step = pl.program_id(0)
    half = step // tiles
    query_stretch = slot_ref[2 * (reach + 1) + half]
    query_first = query_stretch * rows + (step % tiles) * TQ
    lanes = heads * TQ

    @pl.when(step == 0)
    def _():
        def clear(slot, carried):
            acc_ref[slot] = jnp.zeros((rows, 2 * width), jnp.float32)
            return carried

        lax.fori_loop(0, 2 * (reach + 1), clear, 0)

    def heads_first(ref):
        parts = [ref[:, h * width : (h + 1) * width] for h in range(heads)]
        return jnp.concatenate(parts, axis=0) if heads > 1 else parts[0]

    q = heads_first(q_ref)
    do = heads_first(do_ref)
    q_t = q.T
    do_t = do.T
    starts = start_ref[0]
    spread = lax.broadcasted_iota(jnp.int32, (1, lanes), 1) % TQ + query_first - starts
    key_row = lax.broadcasted_iota(jnp.int32, (TK, 1), 0)

    tile_low = first_ref[step] // TK

    def place(tile):
        stretch = tile * TK // rows
        slot = slot_ref[half * (reach + 1) + query_stretch - stretch]
        return slot, pl.multiple_of(tile * TK - stretch * rows, TK)

    def logits2(tile, key_part, masked):
        s = jnp.dot(key_part, q_t, preferred_element_type=jnp.float32) * (scale * LOG2E)
        if not masked:
            return s
        behind = (key_row + tile * TK) - starts
        return jnp.where((behind >= 0) & (behind <= spread), s, MASKED)

    def forward(masked, tile, carried):
        top, total, acc = carried
        slot, row = place(tile)
        key_part = kv_ref[slot, pl.ds(row, TK), :width]
        value_part = kv_ref[slot, pl.ds(row, TK), width:]
        s = logits2(tile, key_part, masked)
        held_ref[tile - tile_low] = s
        new_top = jnp.maximum(top, jnp.max(s, axis=0, keepdims=True))
        p = jnp.exp2(s - new_top)
        shrink = jnp.exp2(top - new_top)
        total = total * shrink + jnp.sum(p, axis=0, keepdims=True)
        acc = acc * shrink + lax.dot_general(
            value_part, p.astype(jnp.bfloat16), (((0,), (0,)), ((), ())), preferred_element_type=jnp.float32
        )
        return new_top, total, acc

    tile_high = (query_first + TQ - 1) // TK + 1
    inner_low = jnp.minimum((last_ref[step] + TK - 1) // TK, tile_high)
    inner_high = jnp.maximum(inner_low, (query_first + 1) // TK)

    def over_tiles(body, carried):
        carried = lax.fori_loop(tile_low, inner_low, functools.partial(body, True), carried)
        carried = lax.fori_loop(inner_low, inner_high, functools.partial(body, False), carried)
        return lax.fori_loop(inner_high, tile_high, functools.partial(body, True), carried)

    top, total, acc = over_tiles(
        forward,
        (
            jnp.full((1, lanes), MASKED, jnp.float32),
            jnp.zeros((1, lanes), jnp.float32),
            jnp.zeros((width, lanes), jnp.float32),
        ),
    )
    out_t = (acc / total).astype(jnp.bfloat16)
    log_total = top + jnp.log2(total)
    delta = jnp.sum(do_t.astype(jnp.float32) * out_t.astype(jnp.float32), axis=0, keepdims=True)
    out = out_t.T
    for h in range(heads):
        out_ref[:, h * width : (h + 1) * width] = out[h * TQ : (h + 1) * TQ]

    def backward(tile, dq_t):
        slot, row = place(tile)
        key_part = kv_ref[slot, pl.ds(row, TK), :width]
        value_part = kv_ref[slot, pl.ds(row, TK), width:]
        p = jnp.exp2(held_ref[tile - tile_low] - log_total)
        dp = jnp.dot(value_part, do_t, preferred_element_type=jnp.float32)
        ds = (p * (dp - delta)).astype(jnp.bfloat16)
        acc_ref[slot, pl.ds(row, TK), :width] += jnp.dot(ds, q, preferred_element_type=jnp.float32)
        acc_ref[slot, pl.ds(row, TK), width:] += jnp.dot(
            p.astype(jnp.bfloat16), do, preferred_element_type=jnp.float32
        )
        return dq_t + lax.dot_general(
            key_part, ds, (((0,), (0,)), ((), ())), preferred_element_type=jnp.float32
        )

    dq_t = lax.fori_loop(tile_low, tile_high, backward, jnp.zeros((width, lanes), jnp.float32))
    dq = (dq_t * scale).astype(jnp.bfloat16).T
    for h in range(heads):
        dq_ref[:, h * width : (h + 1) * width] = dq[h * TQ : (h + 1) * TQ]

    @pl.when(step == 2 * tiles - 1)
    def _():
        def finish(slot, carried):
            dkv_ref[slot] = acc_ref[slot].astype(jnp.bfloat16)
            return carried

        lax.fori_loop(0, 2 * (reach + 1), finish, 0)


def run_attention(queries, grad_out, window, first, last, slots, starts, rows, reach):
    tok_rows, heads, width = queries.shape
    tiles = rows // TQ
    sizes = (heads, width, rows, tiles, reach, 1.0 / width)
    slot_count = window.shape[0]
    row_spec = pl.BlockSpec((TQ, heads * width), lambda t, *_: (t, 0))
    all_spec = pl.BlockSpec((slot_count, rows, 2 * width), lambda t, *_: (0, 0, 0))
    out, dq, dkv = pl.pallas_call(
        functools.partial(attention_kernel, sizes),
        out_shape=(
            jax.ShapeDtypeStruct((tok_rows, heads * width), jnp.bfloat16),
            jax.ShapeDtypeStruct((tok_rows, heads * width), jnp.bfloat16),
            jax.ShapeDtypeStruct(window.shape, jnp.bfloat16),
        ),
        grid_spec=pltpu.PrefetchScalarGridSpec(
            num_scalar_prefetch=3,
            grid=(2 * tiles,),
            in_specs=[
                row_spec,
                row_spec,
                pl.BlockSpec((1, 1, heads * TQ), lambda t, *_: (t, 0, 0)),
                all_spec,
            ],
            out_specs=(row_spec, row_spec, all_spec),
            scratch_shapes=[
                pltpu.VMEM((slot_count, rows, 2 * width), jnp.float32),
                pltpu.VMEM(((MAXDOC - 1 + TQ) // TK + 2, TK, heads * TQ), jnp.float32),
            ],
        ),
        compiler_params=pltpu.CompilerParams(
            dimension_semantics=("arbitrary",), vmem_limit_bytes=56 * 1024 * 1024
        ),
    )(
        first,
        last,
        slots,
        queries.reshape(tok_rows, heads * width),
        grad_out.reshape(tok_rows, heads * width),
        starts,
        window,
    )
    return out.reshape(queries.shape), dq.reshape(queries.shape), dkv


def extra_pairs(n, k):
    pairs = []
    for below in range(1, k):
        if k < 2 * below + 1 and k >= below + 1 and below < n:
            pairs.append((n - k + below, n - 1 - below))
    return pairs


def gather_kernel(n, reach, x_ref, window_ref, send_sem, extra_sem, pass_sem, recv_sem, local_sem):
    here = lax.axis_index("ctx")
    core = here % 2
    sibling = here + 1 - 2 * core
    rows = window_ref.shape[1]
    part_rows = rows // 2

    barrier = pltpu.get_barrier_semaphore()
    for by in range(1, n):
        pl.semaphore_signal(
            barrier, inc=1, device_id={"ctx": (here + by) % n}, device_id_type=pl.DeviceIdType.MESH
        )
    pl.semaphore_wait(barrier, n - 1)

    def slot_of(f, k):
        return f * (reach + 1) + k

    def own(f, p):
        return x_ref.at[pl.ds(f * rows + p * part_rows, part_rows)]

    def into(f, k, p):
        return window_ref.at[slot_of(f, k), pl.ds(p * part_rows, part_rows)]

    def copy(src, f, k, p, sem, device):
        return pltpu.make_async_remote_copy(
            src_ref=src,
            dst_ref=into(f, k, p),
            send_sem=sem,
            recv_sem=recv_sem.at[slot_of(f, k), p],
            device_id={"ctx": device},
            device_id_type=pl.DeviceIdType.MESH,
        )

    locals_ = [
        pltpu.make_async_copy(
            x_ref.at[pl.ds(f * rows, rows)], window_ref.at[slot_of(f, 0)], local_sem.at[f]
        )
        for f in range(2)
    ]
    for c in locals_:
        c.start()

    def near(f, device_core):
        return device_core == f

    direct = []
    for k in range(reach, 0, -1):
        for f in range(2):
            target = here + k if f == 0 else here - k
            valid = target < n if f == 0 else target >= 0
            target_near = near(f, (core + k) % 2)
            for p in range(2):
                sent = jnp.where(
                    target_near, p == 0 or k == reach, p == 1 or k == 1
                )
                direct.append((valid & sent, copy(own(f, p), f, k, p, send_sem.at[slot_of(f, k), p], target)))
        for source, target in extra_pairs(n, k):
            for p in range(2):
                is_near = target % 2 == 1
                if (is_near and (p == 0 or k == reach)) or (not is_near and (p == 1 or source == target + 1)):
                    direct.append(
                        (here == source, copy(own(0, p), 1, k, p, extra_sem.at[k - 1, target % 2, p], target))
                    )
    for when, c in direct:
        pl.when(when)(c.start)

    def has(f, k):
        if f == 0:
            return here - k >= 0
        found = here + k < n
        for source, target in extra_pairs(n, k):
            found = found | (here == target)
        return found

    passed = []
    arrivals = []
    for k in range(1, reach + 1):
        for f in range(2):
            present = has(f, k)
            here_near = near(f, core)
            whole = jnp.where(here_near, k == reach, k == 1)
            for source, target in extra_pairs(n, k) if f == 1 else []:
                if source == target + 1 and target % 2 == 0:
                    whole = whole | (here == target)
            for p in range(2):
                from_source = whole | (here_near == (p == 0))
                next_k = k + 1 if p == 0 else k - 1
                forwards = 1 <= next_k <= reach
                if forwards:
                    c = copy(into(f, k, p), f, next_k, p, pass_sem.at[slot_of(f, k)], sibling)
                    when = present & (here_near == (p == 0)) & jnp.logical_not(whole)
                    arrived = copy(into(f, k, p), f, k, p, pass_sem.at[slot_of(f, k)], sibling)
                    passed.append((when, c, arrived))
                    arrivals.append((present & jnp.logical_not(when), arrived))
                else:
                    arrived = copy(into(f, k, p), f, k, p, pass_sem.at[slot_of(f, k)], sibling)
                    arrivals.append((present, arrived))
    for when, c, arrived in passed:

        @pl.when(when)
        def _():
            arrived.wait_recv()
            c.start()

    for when, arrived in arrivals:
        pl.when(when)(arrived.wait_recv)
    for when, c in direct:
        pl.when(when)(c.wait_send)
    for when, c, arrived in passed:
        pl.when(when)(c.wait_send)
    for c in locals_:
        c.wait()


def gather(packed, n, reach):
    rows, columns = packed.shape[0] // 2, packed.shape[1]
    slots = 2 * (reach + 1)
    return pl.pallas_call(
        functools.partial(gather_kernel, n, reach),
        out_shape=jax.ShapeDtypeStruct((slots, rows, columns), packed.dtype),
        in_specs=[pl.BlockSpec(memory_space=pl.ANY)],
        out_specs=pl.BlockSpec(memory_space=pl.ANY),
        scratch_shapes=[
            pltpu.SemaphoreType.DMA((slots, 2)),
            pltpu.SemaphoreType.DMA((reach, 2, 2)),
            pltpu.SemaphoreType.DMA((slots,)),
            pltpu.SemaphoreType.DMA((slots, 2)),
            pltpu.SemaphoreType.DMA((2,)),
        ],
        compiler_params=pltpu.CompilerParams(collective_id=0, has_side_effects=True),
    )(packed)


def give_back_kernel(
    n, heads, reach, term_ref, key_ref, value_ref,
    land, extra_land, raw_land, mixed, total, outgoing, head_land,
    send_sem, recv_sem, extra_sem, raw_send, raw_recv, head_send, head_recv,
):
    here = lax.axis_index("ctx")
    mine = lax.axis_index("head")
    core = here % 2
    sibling = here + 1 - 2 * core
    rows, columns = term_ref.shape[1], term_ref.shape[2]
    part_rows = rows // 2
    width = columns // 2
    share = 2 * rows // heads

    barrier = pltpu.get_barrier_semaphore()
    for by in range(1, n):
        pl.semaphore_signal(
            barrier, inc=1, device_id={"ctx": (here + by) % n}, device_id_type=pl.DeviceIdType.MESH
        )
    for by in range(1, heads):
        pl.semaphore_signal(
            barrier, inc=1, device_id={"head": (mine + by) % heads}, device_id_type=pl.DeviceIdType.MESH
        )
    pl.semaphore_wait(barrier, n + heads - 2)

    def slot_of(f, k):
        return f * (reach + 1) + k

    def part(p):
        return pl.ds(p * part_rows, part_rows)

    def remote(src, dst, sem, arrival, device):
        return pltpu.make_async_remote_copy(
            src_ref=src, dst_ref=dst, send_sem=sem, recv_sem=arrival,
            device_id={"ctx": device}, device_id_type=pl.DeviceIdType.MESH,
        )

    extras = [(k, a, b) for k in range(1, reach + 1) for a, b in extra_pairs(n, k)]
    raws, straight, mixes = [], [], []
    for k in range(reach, 0, -1):
        for f in range(2):
            slot = slot_of(f, k)
            plain = here - k >= 0 if f == 0 else here + k < n
            back = here - k if f == 0 else here + k
            here_near = core == f
            whole = jnp.where(here_near, k == reach, k == 1)
            routes = [(plain, back, None)]
            present = plain
            for number, (ek, a, b) in enumerate(extras):
                if f == 1 and ek == k:
                    routes.append((here == b, a, number))
                    present = present | (here == b)
                    if a == b + 1 and b % 2 == 0:
                        whole = whole | (here == b)
            shared = present & jnp.logical_not(whole)
            for p in range(2):
                combines = here_near == (p == 0)
                next_k = k - 1 if p == 0 else k + 1
                if 1 <= next_k <= reach:
                    raws.append((
                        shared & jnp.logical_not(combines),
                        remote(
                            term_ref.at[slot, part(p)], raw_land.at[slot_of(f, next_k)],
                            raw_send.at[slot], raw_recv.at[slot_of(f, next_k)], sibling,
                        ),
                    ))
                if 1 <= (k + 1 if p == 0 else k - 1) <= reach:
                    sends = []
                    for when, device, number in routes:
                        dst = land.at[slot, part(p)] if number is None else extra_land.at[number, part(p)]
                        arrival = recv_sem.at[slot, p] if number is None else extra_sem.at[number, p]
                        sends.append((
                            when & shared & combines,
                            remote(mixed.at[slot], dst, send_sem.at[slot, p], arrival, device),
                        ))
                    wait = remote(mixed.at[slot], raw_land.at[slot], raw_send.at[slot], raw_recv.at[slot], sibling)
                    mixes.append((shared & combines, slot, p, wait, sends))
                for when, device, number in routes:
                    dst = land.at[slot, part(p)] if number is None else extra_land.at[number, part(p)]
                    arrival = recv_sem.at[slot, p] if number is None else extra_sem.at[number, p]
                    straight.append((
                        when & whole,
                        remote(term_ref.at[slot, part(p)], dst, send_sem.at[slot, p], arrival, device),
                    ))
    for when, c in raws + straight:
        pl.when(when)(c.start)
    for f in range(2):
        total[pl.ds(f * rows, rows)] = term_ref[slot_of(f, 0)].astype(jnp.float32)
    for when, slot, p, wait, sends in mixes:

        @pl.when(when)
        def _():
            wait.wait_recv()
            mixed[slot] = (
                term_ref[slot, part(p)].astype(jnp.float32) + raw_land[slot].astype(jnp.float32)
            ).astype(jnp.bfloat16)

        for sent, c in sends:
            pl.when(sent)(c.start)

    def add(when, row, buffer, arrival):
        @pl.when(when)
        def _():
            remote(buffer, buffer, raw_send.at[0], arrival, sibling).wait_recv()
            total[pl.ds(row, part_rows)] += buffer[...].astype(jnp.float32)

    for k in range(1, reach + 1):
        for f in range(2):
            target = here + k if f == 0 else here - k
            valid = target < n if f == 0 else target >= 0
            target_near = (core + k) % 2 == f
            for p in range(2):
                sent = jnp.where(target_near, p == 0 or k == reach, p == 1 or k == 1)
                slot = slot_of(f, k)
                add(valid & sent, f * rows + p * part_rows, land.at[slot, part(p)], recv_sem.at[slot, p])
    for number, (k, a, b) in enumerate(extras):
        for p in range(2):
            if b % 2 == 1:
                sent = p == 0 or k == reach
            else:
                sent = p == 1 or a == b + 1
            if sent:
                add(here == a, p * part_rows, extra_land.at[number, part(p)], extra_sem.at[number, p])

    outgoing[...] = total[...].astype(jnp.bfloat16)
    head_copies = []
    for by in range(1, heads):
        other = (mine + by) % heads
        c = pltpu.make_async_remote_copy(
            src_ref=outgoing.at[pl.ds(pl.multiple_of(other * share, share), share)],
            dst_ref=head_land.at[by - 1],
            send_sem=head_send.at[by - 1],
            recv_sem=head_recv.at[by - 1],
            device_id={"head": other},
            device_id_type=pl.DeviceIdType.MESH,
        )
        c.start()
        head_copies.append(c)
    result = total[pl.ds(pl.multiple_of(mine * share, share), share)]
    for by, c in enumerate(head_copies):
        c.wait_recv()
        result = result + head_land[by].astype(jnp.float32)
    key_ref[...] = (result[:, :width] * (1.0 / width)).astype(jnp.bfloat16)
    value_ref[...] = result[:, width:].astype(jnp.bfloat16)
    for when, c in raws + straight:
        pl.when(when)(c.wait_send)
    for when, slot, p, wait, sends in mixes:
        for sent, c in sends:
            pl.when(sent)(c.wait_send)
    for c in head_copies:
        c.wait_send()


def give_back(terms, n, heads, reach):
    slots, rows, columns = terms.shape
    share = 2 * rows // heads
    extras = max(1, sum(len(extra_pairs(n, k)) for k in range(1, reach + 1)))
    low = jnp.bfloat16
    sem = pltpu.SemaphoreType.DMA
    result = jax.ShapeDtypeStruct((share, columns // 2), low)
    return pl.pallas_call(
        functools.partial(give_back_kernel, n, heads, reach),
        out_shape=(result, result),
        in_specs=[pl.BlockSpec(memory_space=pltpu.VMEM)],
        out_specs=(pl.BlockSpec(memory_space=pltpu.VMEM),) * 2,
        scratch_shapes=[
            pltpu.VMEM((slots, rows, columns), low),
            pltpu.VMEM((extras, rows, columns), low),
            pltpu.VMEM((slots, rows // 2, columns), low),
            pltpu.VMEM((slots, rows // 2, columns), low),
            pltpu.VMEM((2 * rows, columns), jnp.float32),
            pltpu.VMEM((2 * rows, columns), low),
            pltpu.VMEM((heads - 1, share, columns), low),
            sem((slots, 2)),
            sem((slots, 2)),
            sem((extras, 2)),
            sem((slots,)),
            sem((slots,)),
            sem((heads - 1,)),
            sem((heads - 1,)),
        ],
        compiler_params=pltpu.CompilerParams(
            collective_id=1, has_side_effects=True, vmem_limit_bytes=50 * 1024 * 1024
        ),
    )(terms)


def per_device(queries, key_vectors, value_vectors, grad_out, doc_lengths):
    n = lax.axis_size("ctx")
    here = lax.axis_index("ctx")
    tok_rows, heads, width = queries.shape
    rows = tok_rows // 2
    reach = (MAXDOC - 1 + rows - 1) // rows
    tiles = rows // TQ
    packed = jnp.concatenate([key_vectors, value_vectors], axis=1)

    window = gather(packed, n, reach)

    steps = jnp.arange(reach + 1, dtype=jnp.int32)
    again = 2 * here - (2 * n - 1) + steps
    slots = jnp.concatenate(
        [
            steps,
            jnp.where((again >= 0) & (again <= reach), again, steps + reach + 1),
            jnp.stack([here, 2 * n - 1 - here]),
        ]
    ).astype(jnp.int32)

    doc_ends = jnp.cumsum(doc_lengths)
    stretch = jnp.stack([here, 2 * n - 1 - here]).astype(jnp.int32)
    pos = (stretch[:, None] * rows + jnp.arange(rows, dtype=jnp.int32)[None, :]).reshape(-1)
    begin = jnp.max(jnp.where(doc_ends[None, :] <= pos[:, None], doc_ends[None, :], 0), axis=1)
    begin = begin.astype(jnp.int32).reshape(2 * tiles, TQ)
    starts = jnp.tile(begin, (1, heads)).reshape(2 * tiles, 1, heads * TQ)
    out, dq, dkv = run_attention(
        queries, grad_out, window, begin[:, 0], begin[:, -1], slots, starts, rows, reach
    )

    grad_keys, grad_values = give_back(dkv, n, lax.axis_size("head"), reach)
    return out, dq, grad_keys, grad_values


def solution(mesh):
    placed = (P("ctx", "head", None), P("ctx", None), P("ctx", None), P("ctx", "head", None), P())
    return jax.shard_map(
        per_device,
        mesh=mesh,
        in_specs=placed,
        out_specs=(
            P("ctx", "head", None),
            P("ctx", "head", None),
            P(("ctx", "head"), None),
            P(("ctx", "head"), None),
        ),
        check_vma=False,
    )
```
